256 devices in a mesh: leaf: 64 (over z, y, core), rhs: 4 (over x).
Axes of the slice: x: 4, y: 4, z: 8, core: 2. Of those that a mesh axis runs over, the one named last changes fastest.
Arguments:
- points: bfloat16 [64, 524288], P('rhs', 'leaf'), may hold values from -6 to 6
- leaf_basis: bfloat16 [2048, 64, 256], P('leaf'), may hold values from -0.375 to 0.375
- local_transfer: bfloat16 [64, 31, 64, 128], P('leaf'), may hold values from -0.625 to 0.625
- top_transfer: bfloat16 [48, 64, 128], replicated, may hold values from -0.625 to 0.625
- leaf_coupling: bfloat16 [3, 2048, 64, 320], P(None, 'leaf'), may hold values from -0.3125 to 0.3125
- root_coupling: bfloat16 [3, 64, 64, 192], P(None, 'leaf'), may hold values from -0.4375 to 0.4375
- upper_coupling: bfloat16 [3, 48, 64, 192], replicated, may hold values from -0.4375 to 0.4375
- near_blocks: bfloat16 [3, 2048, 3, 256, 256], P(None, 'leaf', None, 'rhs'), may hold values from -0.21875 to 0.21875
- near_offset: int32 [2048, 3], P('leaf'), may hold values from -8 to 8, as said below
- far_offset: int32 [2048, 5], P('leaf'), may hold values from -8 to 8, as said below
Outputs:
- applied: bfloat16 [3, 64, 524288], P(None, 'rhs', 'leaf')
The draws below stay inside these ranges and needn't reach their ends.
Inputs may be any that keep to these rules, and one draw needn't show every extreme that they name: `near_offset`: the first entry of each row is 0; the entries of a row are distinct and lie within 8 of 0. `far_offset`: entries are nonzero, distinct within a row, and differ from every entry of the same row of near_offset.
All inputs are finite; a program needn't handle non-finite values.
Results may differ from the reference program's by a relative error of at most 0.025.
Values may be sent and summed in bfloat16 or wider, within the bound.
No kernel may reach another device: no remote copies, remote signals or barrier semaphores. Data moves between devices by JAX's collectives and lax.ppermute only.
A program may use at most 192 MiB of HBM per device.

```python
import jax
import jax.numpy as jnp
from jax import lax

LEAF = 256
RANK = 64
NCOL = 64
OPS = 3
LPD = 32
W = 8
NEAR = 3
FAR = 5
TOPL = 3
NLEAF = 2048
NPTS = 524288
SUP = 48
N_LEAF = 64


def window_shuffle(key):
    leaf_keys = jax.random.split(key, NLEAF)
    candidates = jnp.concatenate([jnp.arange(-W, 0, dtype=jnp.int32), jnp.arange(1, W + 1, dtype=jnp.int32)])
    return jax.vmap(lambda single: jax.random.permutation(single, candidates))(leaf_keys).astype(jnp.int32)


def draw_near_offset(key, part):
    shuffled = window_shuffle(key)
    self_column = jnp.zeros((NLEAF, 1), dtype=jnp.int32)
    return jnp.concatenate([self_column, shuffled[:, :NEAR - 1]], axis=1)


def draw_far_offset(key, part):
    shuffled = window_shuffle(key)
    return shuffled[:, NEAR - 1:NEAR - 1 + FAR]


def steps_of(stream_key, shape, pieces, low, largest):
    loudness = 1.0
    for dim, blocks in pieces:
        heights = jax.random.uniform(jax.random.fold_in(jax.random.fold_in(stream_key, 6), dim), (blocks,), jnp.float32, low / len(pieces), largest / len(pieces))
        loudness = loudness * jnp.repeat(jnp.exp(heights), shape[dim] // blocks).reshape((-1,) + (1,) * (len(shape) - 1 - dim))
    return loudness


def normal_values(stream_key, extent, scale, reach, cuts=(), kind=jnp.bfloat16):
    values = scale * jax.random.normal(stream_key, extent, jnp.float32)
    if cuts:
        values = values * steps_of(stream_key, extent, cuts, -0.22, 0.18)
    return jnp.clip(values, -reach, reach).astype(kind)


def setup_inputs(seed: int = 0) -> dict:
    streams_of = jax.random.split(jax.random.key(seed), 11)
    return {
        "points": normal_values(streams_of[0], (NCOL, NPTS), 1.0, 6.0, ((0, 4), (1, 64))),
        "leaf_basis": normal_values(streams_of[1], (NLEAF, RANK, LEAF), LEAF ** -0.5, 0.375, ((0, 64),)),
        "local_transfer": normal_values(streams_of[2], (N_LEAF, LPD - 1, RANK, 2 * RANK), (3 * RANK // 2) ** -0.5, 0.625, ((0, 64),)),
        "top_transfer": normal_values(streams_of[3], (SUP, RANK, 2 * RANK), (3 * RANK // 2) ** -0.5, 0.625),
        "leaf_coupling": normal_values(streams_of[4], (OPS, NLEAF, RANK, FAR * RANK), (FAR * RANK) ** -0.5, 0.3125, ((1, 64),)),
        "root_coupling": normal_values(streams_of[5], (OPS, N_LEAF, RANK, 3 * RANK), (3 * RANK) ** -0.5, 0.4375, ((1, 64),)),
        "upper_coupling": normal_values(streams_of[6], (OPS, SUP, RANK, 3 * RANK), (3 * RANK) ** -0.5, 0.4375),
        "near_blocks": normal_values(streams_of[7], (OPS, NLEAF, NEAR, LEAF, LEAF), (NEAR * LEAF) ** -0.5, 0.21875, ((1, 64), (3, 4))),
        "near_offset": draw_near_offset(jax.random.fold_in(streams_of[10], 71), 0),
        "far_offset": draw_far_offset(jax.random.fold_in(streams_of[10], 71), 0),
    }


def round_half(values):
    return lax.optimization_barrier(values.astype(jnp.bfloat16))


def pair_up(level_coef, transfer):
    col_count, cluster_count, rank_size = level_coef.shape
    joined = level_coef.reshape(col_count, cluster_count // 2, 2 * rank_size).astype(jnp.float32)
    return round_half(jnp.einsum('cpk,prk->cpr', joined, transfer.astype(jnp.float32)))


def pair_down(field, transfer):
    ops_count, col_count, cluster_count, rank_size = field.shape
    narrow = round_half(field).astype(jnp.float32)
    children = jnp.einsum('ocpr,prk->ocpk', narrow, transfer.astype(jnp.float32))
    return children.reshape(ops_count, col_count, 2 * cluster_count, rank_size)


def cousin_sources(level_coef):
    col_count, cluster_count, rank_size = level_coef.shape
    padded = jnp.pad(level_coef, ((0, 0), (3, 3), (0, 0)))
    clusters = jnp.arange(cluster_count, dtype=jnp.int32)[:, None]
    steps_even = jnp.array([-2, 2, 3], dtype=jnp.int32)[None, :]
    steps_odd = jnp.array([-3, -2, 2], dtype=jnp.int32)[None, :]
    chosen = jnp.where(clusters % 2 == 0, steps_even, steps_odd)
    rows_taken = (3 + clusters + chosen).astype(jnp.int32)
    picked = jnp.take(padded, rows_taken.reshape(-1), axis=1)
    return picked.reshape(col_count, cluster_count, 3 * rank_size)


def reference(points, leaf_basis, local_transfer, top_transfer, leaf_coupling, root_coupling, upper_coupling, near_blocks, near_offset, far_offset):
    col_count = points.shape[0]
    leaf_count = leaf_basis.shape[0]
    leaf_points = points.reshape(col_count, leaf_count, LEAF)
    leaf_coef = round_half(jnp.einsum('cti,tri->ctr', leaf_points.astype(jnp.float32), leaf_basis.astype(jnp.float32)))
    depth_local = LPD.bit_length() - 1
    transfers = []
    current = leaf_coef
    offset = 0
    for height in range(depth_local):
        cluster_count = LPD >> (height + 1)
        transfer = local_transfer[:, offset:offset + cluster_count].reshape(N_LEAF * cluster_count, RANK, 2 * RANK)
        transfers.append(transfer)
        current = pair_up(current, transfer)
        offset += cluster_count
    level_coef = current
    fields = []
    for height in range(TOPL):
        level_size = N_LEAF >> height
        if height == 0:
            coupling = root_coupling
        else:
            first_row = N_LEAF - N_LEAF // 2 ** (height - 1)
            level_coef = pair_up(level_coef, top_transfer[first_row:first_row + level_size])
            coupling = upper_coupling[:, first_row:first_row + level_size]
        sources = cousin_sources(level_coef).astype(jnp.float32)
        fields.append(jnp.einsum('cmk,omrk->ocmr', sources, coupling.astype(jnp.float32)))
    running = fields[TOPL - 1]
    for height in range(TOPL - 1, 0, -1):
        first_row = N_LEAF - N_LEAF // 2 ** (height - 1)
        running = fields[height - 1] + pair_down(running, top_transfer[first_row:first_row + (N_LEAF >> height)])
    for height in reversed(range(depth_local)):
        running = pair_down(running, transfers[height])
    leaf_range = jnp.arange(leaf_count, dtype=jnp.int32)[:, None]
    wide_coef = jnp.pad(leaf_coef, ((0, 0), (W, W), (0, 0)))
    far_index = (W + leaf_range + far_offset).astype(jnp.int32)
    sources = jnp.take(wide_coef, far_index.reshape(-1), axis=1).reshape(col_count, leaf_count, FAR * RANK).astype(jnp.float32)
    coupled = jnp.einsum('ctk,otrk->octr', sources, leaf_coupling.astype(jnp.float32))
    leaf_field = round_half(running + coupled).astype(jnp.float32)
    far_part = jnp.einsum('octr,tri->octi', leaf_field, leaf_basis.astype(jnp.float32))
    wide_points = jnp.pad(leaf_points, ((0, 0), (W, W), (0, 0)))
    near_index = (W + leaf_range + near_offset).astype(jnp.int32)

    def group_near(group):
        start_leaf = (group * LPD).astype(jnp.int32)
        wanted = lax.dynamic_slice_in_dim(near_index, start_leaf, LPD, 0)
        local_sources = jnp.take(wide_points, wanted.reshape(-1), axis=1).reshape(col_count, LPD, NEAR, LEAF).astype(jnp.float32)
        blocks = lax.dynamic_slice_in_dim(near_blocks, start_leaf, LPD, 1).astype(jnp.float32)
        return jnp.einsum('ctkj,otkij->octi', local_sources, blocks)

    grouped = lax.map(group_near, jnp.arange(N_LEAF, dtype=jnp.int32))
    near_part = jnp.transpose(grouped, (1, 2, 0, 3, 4)).reshape(OPS, col_count, leaf_count, LEAF)
    return (far_part + near_part).astype(jnp.bfloat16).reshape(OPS, col_count, leaf_count * LEAF)
```

```python
import functools

import jax
import jax.numpy as jnp
from jax import lax
from jax.experimental import pallas as pl
from jax.experimental.pallas import tpu as pltpu
from jax.sharding import PartitionSpec as P

LEAF = 256
RANK = 64
OPS = 3
W = 8
NEAR = 3
FAR = 5
COLS = 16
LEAVES = 32
ROOTS = 64
SIDES = 4
PAIRS = LEAVES // 2

NT = (((1,), (1,)), ((), ()))
NN = (((1,), (0,)), ((), ()))
F32 = jnp.float32
BF16 = jnp.bfloat16

VMEM = pl.BlockSpec(memory_space=pltpu.VMEM)
SMEM = pl.BlockSpec(memory_space=pltpu.SMEM)
ANY = pl.BlockSpec(memory_space=pl.ANY)


def dot_nt(a, b):
    return lax.dot_general(a, b, NT, preferred_element_type=F32)


def dot_nn(a, b):
    return lax.dot_general(a, b, NN, preferred_element_type=F32)


def params(mib):
    return pltpu.CompilerParams(vmem_limit_bytes=mib * 2**20)


def cost(flops, bytes_accessed):
    return pl.CostEstimate(flops=flops, bytes_accessed=bytes_accessed, transcendentals=0)


def up_kernel(points_ref, basis_ref, transfer_ref, pairs_ref, root_ref):
    level = []
    for pair in range(PAIRS):
        halves = [
            dot_nt(points_ref[:, t * LEAF : (t + 1) * LEAF], basis_ref[t])
            for t in (2 * pair, 2 * pair + 1)
        ]
        joined = jnp.concatenate(halves, axis=1).astype(BF16)
        pairs_ref[pair] = joined
        level.append(joined)
    first = 0
    while True:
        parents = [dot_nt(joined, transfer_ref[first + i]) for i, joined in enumerate(level)]
        first += len(level)
        if len(parents) == 1:
            break
        level = [
            jnp.concatenate(parents[i : i + 2], axis=1).astype(BF16)
            for i in range(0, len(parents), 2)
        ]
    root = parents[0].astype(BF16)
    for slot in range(ROOTS):
        root_ref[slot * COLS : (slot + 1) * COLS] = root


def upsweep(points, leaf_basis, transfer):
    return pl.pallas_call(
        up_kernel,
        in_specs=[VMEM] * 3,
        out_specs=[VMEM] * 2,
        out_shape=[
            jax.ShapeDtypeStruct((PAIRS, COLS, 2 * RANK), BF16),
            jax.ShapeDtypeStruct((ROOTS * COLS, RANK), BF16),
        ],
        compiler_params=params(8),
        cost_estimate=cost(2**25, 2**21),
        name="upsweep",
    )(points, leaf_basis, transfer)


def near_leaf(sources, blocks_ref, t):
    wide = jnp.concatenate(sources, axis=1)
    block = jnp.concatenate(
        [blocks_ref[:, t, k].reshape(OPS * RANK, LEAF) for k in range(NEAR)], axis=1
    )
    return dot_nt(wide, block)


def store_pair(out_refs, slot, results):
    both = jnp.concatenate(results, axis=1).astype(BF16)
    for side, out_ref in enumerate(out_refs):
        out_ref[slot * COLS : (slot + 1) * COLS] = both[side * COLS : (side + 1) * COLS]


def inner_kernel(offset_ref, p0, p1, p2, p3, blocks_ref, *out_refs):
    for pair in range(W // 2, PAIRS - W // 2):
        results = []
        for t in (2 * pair, 2 * pair + 1):
            sources = []
            for k in range(NEAR):
                start = pl.multiple_of((t + offset_ref[t, k]) * LEAF, LEAF)
                sources.append(
                    jnp.concatenate([p[:, pl.ds(start, LEAF)] for p in (p0, p1, p2, p3)], axis=0)
                )
            results.append(near_leaf(sources, blocks_ref, t))
        store_pair(out_refs, pair - W // 2, results)


def outer_kernel(offset_ref, p0, p1, p2, p3, left_ref, right_ref, blocks_ref, *refs):
    out_refs, window = refs[:SIDES], refs[SIDES]
    span = W * LEAF
    for side, part in enumerate((0, 1)):
        base = part * (LEAVES - 2 * W) * LEAF
        halo_at, own_at = (0, span) if part == 0 else (2 * span, 0)
        halo_ref = left_ref if part == 0 else right_ref
        window[side, :, halo_at : halo_at + span] = halo_ref[:, :span]
        for row, p in enumerate((p0, p1, p2, p3)):
            window[side, row * COLS : (row + 1) * COLS, own_at : own_at + 2 * span] = p[
                :, base : base + 2 * span
            ]
    slot = 0
    for part in (0, 1):
        for pair in range(W // 2):
            results = []
            for e in (0, 1):
                local = 2 * pair + e
                t = local + part * (LEAVES - W)
                sources = []
                for k in range(NEAR):
                    start = pl.multiple_of((W + local + offset_ref[t, k]) * LEAF, LEAF)
                    sources.append(window[part, :, pl.ds(start, LEAF)])
                results.append(near_leaf(sources, blocks_ref, t))
            store_pair(out_refs, slot, results)
            slot += 1


NEAR_OUT = [jax.ShapeDtypeStruct((PAIRS // 2 * COLS, 6 * RANK), BF16)] * SIDES


def near_inner(offsets, pieces, blocks):
    return pl.pallas_call(
        inner_kernel,
        in_specs=[SMEM] + [VMEM] * 5,
        out_specs=[VMEM] * SIDES,
        out_shape=NEAR_OUT,
        compiler_params=params(16),
        cost_estimate=cost(2**28, 2**23),
        name="near_inner",
    )(offsets, *pieces, blocks)


def near_outer(offsets, pieces, left, right, blocks):
    return pl.pallas_call(
        outer_kernel,
        in_specs=[SMEM] + [VMEM] * 7,
        out_specs=[VMEM] * SIDES,
        out_shape=NEAR_OUT,
        scratch_shapes=[pltpu.VMEM((2, SIDES * COLS, 3 * W * LEAF), BF16)],
        compiler_params=params(16),
        cost_estimate=cost(2**28, 2**23),
        name="near_outer",
    )(offsets, *pieces, left, right, blocks)


def by_operator(flat):
    return jnp.concatenate([flat[:, o * RANK : (o + 1) * RANK] for o in range(OPS)], axis=0)


def half_of(children, odd):
    return jnp.where(odd == 1, children[:, RANK:], children[:, :RANK])


def far_kernel(
    where_ref,
    offset_ref,
    roots_ref,
    top_ref,
    root_coupling_ref,
    upper_ref,
    transfer_ref,
    pairs_ref,
    left_ref,
    right_ref,
    coupling_ref,
    basis_ref,
    out_ref,
    upper1,
    upper2,
    near_coef,
    sems,
):
    q = where_ref[0]
    copies = []
    for slot, (level, buffer) in enumerate(((1, upper1), (2, upper2))):
        row = (0, ROOTS // 2)[level - 1] + (q >> level)
        copy = pltpu.make_async_copy(upper_ref.at[:, row], buffer, sems.at[slot])
        copy.start()
        copies.append(copy)

    def spread(first, source):
        for i in range(source.shape[0] // COLS):
            both = source[i * COLS : (i + 1) * COLS, :]
            near_coef[first + 2 * i] = both[:, :RANK]
            near_coef[first + 2 * i + 1] = both[:, RANK:]

    spread(0, left_ref[:, W * LEAF :])
    spread(W, pairs_ref[...].reshape(PAIRS * COLS, 2 * RANK))
    spread(W + LEAVES, right_ref[:, W * LEAF :])

    def valid(c, height):
        return jnp.logical_and(c >= 0, c < (ROOTS >> height))

    def clip(c, height):
        return jnp.minimum(jnp.maximum(c, 0), (ROOTS >> height) - 1)

    def coef(height, c):
        if height == 0:
            return roots_ref[c]
        first = (0, ROOTS // 2)[height - 1]
        joined = jnp.concatenate([coef(height - 1, 2 * c), coef(height - 1, 2 * c + 1)], axis=1)
        return dot_nt(joined, top_ref[first + c]).astype(BF16)

    def sources(height):
        c = q >> height
        odd = c % 2
        parts = []
        for even_step, odd_step in ((-2, -3), (2, -2), (3, 2)):
            other = c + jnp.where(odd == 1, odd_step, even_step)
            value = coef(height, clip(other, height))
            parts.append(jnp.where(valid(other, height), value, jnp.zeros_like(value)))
        return jnp.concatenate(parts, axis=1)

    fields = [dot_nt(sources(0), root_coupling_ref[:, 0].reshape(OPS * RANK, 3 * RANK))]
    wide1, wide2 = sources(1), sources(2)
    copies[0].wait()
    copies[1].wait()
    fields.append(dot_nt(wide1, upper1[...].reshape(OPS * RANK, 3 * RANK)))
    fields.append(dot_nt(wide2, upper2[...].reshape(OPS * RANK, 3 * RANK)))

    running = by_operator(fields[2])
    children = dot_nn(running.astype(BF16), top_ref[ROOTS // 2 + (q >> 2)])
    running = by_operator(fields[1]) + half_of(children, (q >> 1) % 2)
    children = dot_nn(running.astype(BF16), top_ref[q >> 1])
    running = by_operator(fields[0]) + half_of(children, q % 2)

    level = [running]
    last = LEAVES - 1
    while len(level) < LEAVES:
        count = len(level)
        last -= count
        lower = []
        for i, value in enumerate(level):
            children = dot_nn(value.astype(BF16), transfer_ref[last + i])
            lower += [children[:, :RANK], children[:, RANK:]]
        level = lower

    for t in range(LEAVES):
        wide = jnp.concatenate([near_coef[W + t + offset_ref[t, k]] for k in range(FAR)], axis=1)
        coupled = dot_nt(wide, coupling_ref[:, t].reshape(OPS * RANK, FAR * RANK))
        field = (level[t] + by_operator(coupled)).astype(BF16)
        far = dot_nn(field, basis_ref[t])
        out_ref[:, :, t * LEAF : (t + 1) * LEAF] = far.reshape(OPS, COLS, LEAF)


def far_field(where, offsets, roots, top, root_coupling, upper, transfer, pairs, left, right, coupling, basis):
    return pl.pallas_call(
        far_kernel,
        in_specs=[SMEM, SMEM, VMEM, VMEM, VMEM, ANY] + [VMEM] * 6,
        out_specs=VMEM,
        out_shape=jax.ShapeDtypeStruct((OPS, COLS, LEAVES * LEAF), F32),
        scratch_shapes=[
            pltpu.VMEM((OPS, RANK, 3 * RANK), BF16),
            pltpu.VMEM((OPS, RANK, 3 * RANK), BF16),
            pltpu.VMEM((LEAVES + 2 * W, COLS, RANK), BF16),
            pltpu.SemaphoreType.DMA((2,)),
        ],
        compiler_params=params(16),
        cost_estimate=cost(2**27, 2**23),
        name="far_field",
    )(where, offsets, roots, top, root_coupling, upper, transfer, pairs, left, right, coupling, basis)


def join_kernel(where_ref, far_ref, *refs):
    inner, outer = refs[:SIDES], refs[SIDES : 2 * SIDES]
    out_ref, ordered = refs[2 * SIDES :]
    me = where_ref[0]
    half = PAIRS // 2 * COLS
    edge = W // 2 * COLS
    for step in range(SIDES):
        rows = lax.rem(me + SIDES - step, SIDES)
        ordered[rows, :edge] = outer[step][:edge]
        ordered[rows, edge : edge + half] = inner[step][...]
        ordered[rows, edge + half :] = outer[step][edge:]
    for pair in range(PAIRS):
        parts = [ordered[r, pair * COLS : (pair + 1) * COLS].astype(F32) for r in range(SIDES)]
        for e in (0, 1):
            for o in range(OPS):
                at = (e * OPS + o) * RANK
                near = jnp.concatenate([part[:, at : at + RANK] for part in parts], axis=1)
                columns = slice((2 * pair + e) * LEAF, (2 * pair + e + 1) * LEAF)
                out_ref[o, :, columns] = (far_ref[o, :, columns] + near).astype(BF16)


def join(where, far, inner, outer):
    return pl.pallas_call(
        join_kernel,
        in_specs=[SMEM] + [VMEM] * (1 + 2 * SIDES),
        out_specs=VMEM,
        out_shape=jax.ShapeDtypeStruct((OPS, COLS, LEAVES * LEAF), BF16),
        scratch_shapes=[pltpu.VMEM((SIDES, PAIRS * COLS, 6 * RANK), BF16)],
        compiler_params=params(8),
        cost_estimate=cost(2**20, 2**22),
        name="join",
    )(where, far, *inner, *outer)


def round_rhs(value, step):
    return lax.ppermute(value, "rhs", [(i, (i + step) % SIDES) for i in range(SIDES)])


def along_leaf(value, step):
    count = lax.axis_size("leaf")
    return lax.ppermute(
        value, "leaf", [(i, i + step) for i in range(count) if 0 <= i + step < count]
    )


def per_device(
    points,
    leaf_basis,
    local_transfer,
    top_transfer,
    leaf_coupling,
    root_coupling,
    upper_coupling,
    near_blocks,
    near_offset,
    far_offset,
):
    leaf_index = lax.axis_index("leaf").astype(jnp.int32).reshape(1)
    rhs_index = lax.axis_index("rhs").astype(jnp.int32).reshape(1)
    transfer = local_transfer[0]

    pieces = [points] + [round_rhs(points, -step) for step in range(1, SIDES)]
    pairs, root = upsweep(points, leaf_basis, transfer)
    roots = lax.all_to_all(root, "leaf", 0, 0, tiled=True).reshape(ROOTS, COLS, RANK)

    edge = W * LEAF
    tail = jnp.concatenate(
        [
            jnp.concatenate([p[:, -edge:] for p in pieces], axis=0),
            pairs[-W // 2 :].reshape(SIDES * COLS, 2 * RANK),
        ],
        axis=1,
    )
    head = jnp.concatenate(
        [
            jnp.concatenate([p[:, :edge] for p in pieces], axis=0),
            pairs[: W // 2].reshape(SIDES * COLS, 2 * RANK),
        ],
        axis=1,
    )
    left = along_leaf(tail, 1)
    right = along_leaf(head, -1)

    inner = near_inner(near_offset, pieces, near_blocks)
    inner = [inner[0]] + [round_rhs(inner[step], step) for step in range(1, SIDES)]
    outer = near_outer(near_offset, pieces, left, right, near_blocks)
    outer = [outer[0]] + [round_rhs(outer[step], step) for step in range(1, SIDES)]
    far = far_field(
        leaf_index,
        far_offset,
        roots,
        top_transfer,
        root_coupling,
        upper_coupling,
        transfer,
        pairs,
        left,
        right,
        leaf_coupling,
        leaf_basis,
    )
    return join(rhs_index, far, inner, outer)


def solution(mesh):
    placed = (
        P("rhs", "leaf"),
        P("leaf", None, None),
        P("leaf", None, None, None),
        P(),
        P(None, "leaf", None, None),
        P(None, "leaf", None, None),
        P(),
        P(None, "leaf", None, "rhs", None),
        P("leaf", None),
        P("leaf", None),
    )
    return jax.shard_map(
        per_device, mesh=mesh, in_specs=placed, out_specs=P(None, "rhs", "leaf"), check_vma=False
    )
```

```python
import functools

import jax
import jax.numpy as jnp
from jax import lax
from jax.experimental import pallas as pl
from jax.experimental.pallas import tpu as pltpu
from jax.sharding import PartitionSpec as P

LEAF = 256
RANK = 64
OPS = 3
W = 8
NEAR = 3
FAR = 5
TOPL = 3
COLS = 16
LEAVES = 32
ROOTS = 64
WINDOW = 32
SIDES = 4
PAIRS = LEAVES // 2
HALO = W * LEAF + 2 * RANK

NT = (((1,), (1,)), ((), ()))
NN = (((1,), (0,)), ((), ()))
F32 = jnp.float32
BF16 = jnp.bfloat16

VMEM = pl.BlockSpec(memory_space=pltpu.VMEM)
SMEM = pl.BlockSpec(memory_space=pltpu.SMEM)
ANY = pl.BlockSpec(memory_space=pl.ANY)
HBM = pl.BlockSpec(memory_space=pltpu.HBM)


def dot_nt(a, b):
    return lax.dot_general(a, b, NT, preferred_element_type=F32)


def dot_nn(a, b):
    return lax.dot_general(a, b, NN, preferred_element_type=F32)


def params(mib):
    return pltpu.CompilerParams(vmem_limit_bytes=mib * 2**20)


def in_hbm(value):
    return pltpu.with_memory_space_constraint(value, pltpu.HBM)


def cost(flops, bytes_accessed):
    return pl.CostEstimate(flops=flops, bytes_accessed=bytes_accessed, transcendentals=0)


def like(shape, dtype=BF16):
    return jax.ShapeDtypeStruct(shape, dtype)


class Staged:
    def __init__(self, moves, sems, ahead):
        self.copies = [pltpu.make_async_copy(a, b, sems.at[i]) for i, (a, b) in enumerate(moves)]
        self.started = 0
        self.waited = 0
        self.ahead = ahead
        self.fill()

    def fill(self):
        while self.started < min(len(self.copies), self.waited + self.ahead):
            self.copies[self.started].start()
            self.started += 1

    def wait(self, upto):
        while self.waited <= upto:
            self.copies[self.waited].wait()
            self.waited += 1
            self.fill()


UP_CUT = 16


def up_kernel(points_hbm, basis_hbm, transfer_hbm, pairs_ref, root_ref, points, basis, transfer, sems):
    moves = [(points_hbm, points)]
    for first in range(0, LEAVES, UP_CUT):
        rows = pl.ds(first, UP_CUT)
        moves.append((basis_hbm.at[rows], basis.at[rows]))
    moves.append((transfer_hbm, transfer))
    staged = Staged(moves, sems, 8)
    level = []
    for pair in range(PAIRS):
        staged.wait(1 + 2 * pair // UP_CUT)
        halves = [
            dot_nt(points[:, t * LEAF : (t + 1) * LEAF], basis[t])
            for t in (2 * pair, 2 * pair + 1)
        ]
        joined = jnp.concatenate(halves, axis=1).astype(BF16)
        pairs_ref[pair * COLS : (pair + 1) * COLS] = joined
        level.append(joined)
    staged.wait(len(moves) - 1)
    first = 0
    while True:
        parents = [dot_nt(joined, transfer[first + i]) for i, joined in enumerate(level)]
        first += len(level)
        if len(parents) == 1:
            break
        level = [
            jnp.concatenate(parents[i : i + 2], axis=1).astype(BF16)
            for i in range(0, len(parents), 2)
        ]
    root_ref[0] = parents[0].astype(BF16)


def upsweep(points, leaf_basis, transfer):
    return pl.pallas_call(
        up_kernel,
        in_specs=[HBM] * 3,
        out_specs=[VMEM] * 2,
        out_shape=[like((PAIRS * COLS, 2 * RANK)), like((1, COLS, RANK))],
        scratch_shapes=[
            pltpu.VMEM(points.shape, BF16),
            pltpu.VMEM(leaf_basis.shape, BF16),
            pltpu.VMEM(transfer.shape, BF16),
            pltpu.SemaphoreType.DMA((2 + LEAVES // UP_CUT,)),
        ],
        compiler_params=params(8),
        cost_estimate=cost(2**33, 2**20),
        name="upsweep",
    )(in_hbm(points), in_hbm(leaf_basis), in_hbm(transfer))


def pack_kernel(p0, p1, p2, p3, pairs_ref, after_ref, head_ref, tail_ref):
    del after_ref
    span = W * LEAF
    for row, p in enumerate((p0, p1, p2, p3)):
        rows = slice(row * COLS, (row + 1) * COLS)
        head_ref[rows, :span] = p[:, :span]
        tail_ref[rows, :span] = p[:, LEAVES * LEAF - span :]
    edge = W // 2 * COLS
    head_ref[:, span:] = pairs_ref[:edge]
    tail_ref[:, span:] = pairs_ref[PAIRS * COLS - edge :]


def pack_halos(pieces, pairs, after):
    return pl.pallas_call(
        pack_kernel,
        in_specs=[VMEM] * (SIDES + 1) + [ANY],
        out_specs=[VMEM] * 2,
        out_shape=[like((SIDES * COLS, HALO))] * 2,
        compiler_params=params(4),
        cost_estimate=cost(2**33, 2**20),
        name="pack_halos",
    )(*pieces, pairs, after)


def append_kernel(first_ref, second_ref, after_ref, out_ref):
    del after_ref
    count = first_ref.shape[0]
    out_ref[:count] = first_ref[...]
    out_ref[count:] = second_ref[...]


def append(first, second, after):
    return pl.pallas_call(
        append_kernel,
        in_specs=[VMEM] * 2 + [ANY],
        out_specs=VMEM,
        out_shape=like((2 * first.shape[0], COLS, RANK)),
        compiler_params=params(4),
        cost_estimate=cost(0, 0),
        name="append",
    )(first, second, after)


def near_leaf(sources, blocks_ref, t):
    wide = jnp.concatenate(sources, axis=1)
    block = jnp.concatenate(
        [blocks_ref[:, t, k].reshape(OPS * RANK, LEAF) for k in range(NEAR)], axis=1
    )
    return dot_nt(wide, block)


def store_pair(out_refs, slot, results):
    both = jnp.concatenate(results, axis=1).astype(BF16)
    for side, out_ref in enumerate(out_refs):
        out_ref[slot * COLS : (slot + 1) * COLS] = both[side * COLS : (side + 1) * COLS]


def near_kernel(offset_ref, p0, p1, p2, p3, left_ref, right_ref, blocks_ref, after_ref, *refs):
    del after_ref
    out_refs, window = refs[:SIDES], refs[SIDES]
    span, own = W * LEAF, LEAVES * LEAF
    window[:, :span] = left_ref[:, :span]
    window[:, span + own :] = right_ref[:, :span]
    for row, p in enumerate((p0, p1, p2, p3)):
        window[row * COLS : (row + 1) * COLS, span : span + own] = p[...]
    for pair in range(PAIRS):
        results = []
        for t in (2 * pair, 2 * pair + 1):
            sources = []
            for k in range(NEAR):
                start = pl.multiple_of((W + t + offset_ref[k, t]) * LEAF, LEAF)
                sources.append(window[:, pl.ds(start, LEAF)])
            results.append(near_leaf(sources, blocks_ref, t))
        store_pair(out_refs, pair, results)


def near_field(offsets, pieces, left, right, blocks, after):
    return pl.pallas_call(
        near_kernel,
        in_specs=[SMEM] + [VMEM] * 7 + [ANY],
        out_specs=[VMEM] * SIDES,
        out_shape=[like((PAIRS * COLS, 6 * RANK))] * SIDES,
        scratch_shapes=[pltpu.VMEM((SIDES * COLS, (LEAVES + 2 * W) * LEAF), BF16)],
        compiler_params=params(8),
        cost_estimate=cost(6 * 10**9, 2**22),
        name="near_field",
    )(offsets, *pieces, left, right, blocks, after)


def by_operator(flat):
    return jnp.concatenate([flat[:, o * RANK : (o + 1) * RANK] for o in range(OPS)], axis=0)


def half_of(children, odd):
    return jnp.where(odd == 1, children[:, RANK:], children[:, :RANK])


def couple_kernel(offset_ref, pairs_ref, left_ref, right_ref, coupling_ref, out_ref, near_coef):
    def spread(first, source):
        for i in range(source.shape[0] // COLS):
            both = source[i * COLS : (i + 1) * COLS, :]
            near_coef[first + 2 * i] = both[:, :RANK]
            near_coef[first + 2 * i + 1] = both[:, RANK:]

    spread(0, left_ref[:, W * LEAF :])
    spread(W, pairs_ref[...])
    spread(W + LEAVES, right_ref[:, W * LEAF :])
    for t in range(LEAVES):
        wide = jnp.concatenate([near_coef[W + t + offset_ref[k, t]] for k in range(FAR)], axis=1)
        out_ref[t] = by_operator(dot_nt(wide, coupling_ref[:, t].reshape(OPS * RANK, FAR * RANK)))


def couple_leaves(offsets, pairs, left, right, coupling):
    return pl.pallas_call(
        couple_kernel,
        in_specs=[SMEM] + [VMEM] * 4,
        out_specs=VMEM,
        out_shape=like((LEAVES, OPS * COLS, RANK), F32),
        scratch_shapes=[pltpu.VMEM((LEAVES + 2 * W, COLS, RANK), BF16)],
        compiler_params=params(8),
        cost_estimate=cost(3 * 10**9, 2**22),
        name="couple_leaves",
    )(offsets, pairs, left, right, coupling)


def far_kernel(
    where_ref,
    roots_ref,
    coupled_ref,
    root_ref,
    upper_hbm,
    top_ref,
    transfer_ref,
    basis_ref,
    out_ref,
    upper1,
    upper2,
    sems,
):
    q = where_ref[0]
    staged = Staged(
        [(upper_hbm.at[:, q >> 1], upper1), (upper_hbm.at[:, ROOTS // 2 + (q >> 2)], upper2)], sems, 2
    )

    def valid(c, height):
        return jnp.logical_and(c >= 0, c < (ROOTS >> height))

    def clip(c, height):
        return jnp.minimum(jnp.maximum(c, 0), (ROOTS >> height) - 1)

    def coef(height, c):
        if height == 0:
            return roots_ref[c - q + WINDOW // 2]
        first = (0, ROOTS // 2)[height - 1]
        joined = jnp.concatenate([coef(height - 1, 2 * c), coef(height - 1, 2 * c + 1)], axis=1)
        return dot_nt(joined, top_ref[first + c]).astype(BF16)

    def sources(height):
        c = q >> height
        odd = c % 2
        parts = []
        for even_step, odd_step in ((-2, -3), (2, -2), (3, 2)):
            other = c + jnp.where(odd == 1, odd_step, even_step)
            value = coef(height, clip(other, height))
            parts.append(jnp.where(valid(other, height), value, jnp.zeros_like(value)))
        return jnp.concatenate(parts, axis=1)

    wides = [sources(height) for height in range(TOPL)]
    staged.wait(1)
    couplings = [root_ref[:, 0], upper1[...], upper2[...]]
    fields = [
        dot_nt(wide, coupling.reshape(OPS * RANK, 3 * RANK))
        for wide, coupling in zip(wides, couplings)
    ]
    running = by_operator(fields[2])
    children = dot_nn(running.astype(BF16), top_ref[ROOTS // 2 + (q >> 2)])
    running = by_operator(fields[1]) + half_of(children, (q >> 1) % 2)
    children = dot_nn(running.astype(BF16), top_ref[q >> 1])
    running = by_operator(fields[0]) + half_of(children, q % 2)

    level = [running]
    last = LEAVES - 1
    while len(level) < LEAVES:
        count = len(level)
        last -= count
        lower = []
        for i, value in enumerate(level):
            children = dot_nn(value.astype(BF16), transfer_ref[last + i])
            lower += [children[:, :RANK], children[:, RANK:]]
        level = lower

    for t in range(LEAVES):
        far = dot_nn((level[t] + coupled_ref[t]).astype(BF16), basis_ref[t])
        out_ref[:, :, t * LEAF : (t + 1) * LEAF] = far.reshape(OPS, COLS, LEAF)


def far_field(where, roots, coupled, root_coupling, upper, top, transfer, basis):
    return pl.pallas_call(
        far_kernel,
        in_specs=[SMEM] + [VMEM] * 3 + [HBM] + [VMEM] * 3,
        out_specs=VMEM,
        out_shape=like((OPS, COLS, LEAVES * LEAF), F32),
        scratch_shapes=[
            pltpu.VMEM((OPS, RANK, 3 * RANK), BF16),
            pltpu.VMEM((OPS, RANK, 3 * RANK), BF16),
            pltpu.SemaphoreType.DMA((2,)),
        ],
        compiler_params=params(8),
        cost_estimate=cost(3 * 10**9, 2**22),
        name="far_field",
    )(where, roots, coupled, root_coupling, in_hbm(upper), top, transfer, basis)


def join_kernel(where_ref, far_ref, n0, n1, n2, n3, out_ref, ordered):
    me = where_ref[0]
    for step, near in enumerate((n0, n1, n2, n3)):
        ordered[lax.rem(me + SIDES - step, SIDES)] = near[...]
    for pair in range(PAIRS):
        parts = [ordered[r, pair * COLS : (pair + 1) * COLS].astype(F32) for r in range(SIDES)]
        for e in (0, 1):
            for o in range(OPS):
                at = (e * OPS + o) * RANK
                near = jnp.concatenate([part[:, at : at + RANK] for part in parts], axis=1)
                columns = slice((2 * pair + e) * LEAF, (2 * pair + e + 1) * LEAF)
                out_ref[o, :, columns] = (far_ref[o, :, columns] + near).astype(BF16)


def join(where, far, near):
    return pl.pallas_call(
        join_kernel,
        in_specs=[SMEM] + [VMEM] * (1 + SIDES),
        out_specs=VMEM,
        out_shape=jax.ShapeDtypeStruct((OPS, COLS, LEAVES * LEAF), BF16),
        scratch_shapes=[pltpu.VMEM((SIDES, PAIRS * COLS, 6 * RANK), BF16)],
        compiler_params=params(8),
        cost_estimate=cost(2**20, 2**22),
        name="join",
    )(where, far, *near)


def round_rhs(value, step):
    return lax.ppermute(value, "rhs", [(i, (i + step) % SIDES) for i in range(SIDES)])


def round_leaf(value, step):
    count = lax.axis_size("leaf")
    return lax.ppermute(value, "leaf", [(i, (i + step) % count) for i in range(count)])


def along_leaf(value, step):
    count = lax.axis_size("leaf")
    return lax.ppermute(
        value, "leaf", [(i, i + step) for i in range(count) if 0 <= i + step < count]
    )


def per_device(
    points,
    leaf_basis,
    local_transfer,
    top_transfer,
    leaf_coupling,
    root_coupling,
    upper_coupling,
    near_blocks,
    near_offset,
    far_offset,
):
    leaf_index = lax.axis_index("leaf").astype(jnp.int32).reshape(1)
    rhs_index = lax.axis_index("rhs").astype(jnp.int32).reshape(1)

    def grow(roots, after=None):
        more = round_leaf(roots, -roots.shape[0])
        return append(roots, more, roots if after is None else after)

    transfer = local_transfer[0]
    pieces = [points] + [round_rhs(points, -step) for step in range(1, SIDES)]
    pairs, root = upsweep(points, leaf_basis, transfer)
    roots = grow(grow(root))
    head, tail = pack_halos(pieces, pairs, roots)
    left = along_leaf(tail, 1)
    right = along_leaf(head, -1)
    near = near_field(near_offset.T, pieces, left, right, near_blocks, roots)
    roots = grow(roots, near[0])
    roots = grow(roots)
    near = [near[0]] + [round_rhs(near[step], step) for step in range(1, SIDES)]
    coupled = couple_leaves(far_offset.T, pairs, left, right, leaf_coupling)
    roots = append(round_leaf(roots, WINDOW // 2), roots, coupled)
    far = far_field(
        leaf_index, roots, coupled, root_coupling, upper_coupling, top_transfer, transfer, leaf_basis
    )
    return join(rhs_index, far, near)


def solution(mesh):
    placed = (
        P("rhs", "leaf"),
        P("leaf", None, None),
        P("leaf", None, None, None),
        P(),
        P(None, "leaf", None, None),
        P(None, "leaf", None, None),
        P(),
        P(None, "leaf", None, "rhs", None),
        P("leaf", None),
        P("leaf", None),
    )
    return jax.shard_map(
        per_device, mesh=mesh, in_specs=placed, out_specs=P(None, "rhs", "leaf"), check_vma=False
    )
```

```python
import functools

import jax
import jax.numpy as jnp
from jax import lax
from jax.experimental import pallas as pl
from jax.experimental.pallas import tpu as pltpu
from jax.sharding import PartitionSpec as P

LEAF = 256
RANK = 64
OPS = 3
W = 8
NEAR = 3
FAR = 5
TOPL = 3
COLS = 16
LEAVES = 32
ROOTS = 64
WINDOW = 32
SIDES = 4
PAIRS = LEAVES // 2
HALO = W * LEAF + 2 * RANK

NT = (((1,), (1,)), ((), ()))
NN = (((1,), (0,)), ((), ()))
F32 = jnp.float32
BF16 = jnp.bfloat16

VMEM = pl.BlockSpec(memory_space=pltpu.VMEM)
SMEM = pl.BlockSpec(memory_space=pltpu.SMEM)
ANY = pl.BlockSpec(memory_space=pl.ANY)
HBM = pl.BlockSpec(memory_space=pltpu.HBM)


def dot_nt(a, b):
    return lax.dot_general(a, b, NT, preferred_element_type=F32)


def dot_nn(a, b):
    return lax.dot_general(a, b, NN, preferred_element_type=F32)


def params(mib):
    return pltpu.CompilerParams(vmem_limit_bytes=mib * 2**20)


def in_hbm(value):
    return pltpu.with_memory_space_constraint(value, pltpu.HBM)


def cost(flops, bytes_accessed):
    return pl.CostEstimate(flops=flops, bytes_accessed=bytes_accessed, transcendentals=0)


def like(shape, dtype=BF16):
    return jax.ShapeDtypeStruct(shape, dtype)


class Staged:
    def __init__(self, moves, sems, ahead):
        self.copies = [pltpu.make_async_copy(a, b, sems.at[i]) for i, (a, b) in enumerate(moves)]
        self.started = 0
        self.waited = 0
        self.ahead = ahead
        self.fill()

    def fill(self):
        while self.started < min(len(self.copies), self.waited + self.ahead):
            self.copies[self.started].start()
            self.started += 1

    def wait(self, upto):
        while self.waited <= upto:
            self.copies[self.waited].wait()
            self.waited += 1
            self.fill()


UP_CUT = 16


def up_kernel(points_hbm, basis_hbm, transfer_hbm, pairs_ref, root_ref, points, basis, transfer, sems):
    moves = [(points_hbm, points)]
    for first in range(0, LEAVES, UP_CUT):
        rows = pl.ds(first, UP_CUT)
        moves.append((basis_hbm.at[rows], basis.at[rows]))
    moves.append((transfer_hbm, transfer))
    staged = Staged(moves, sems, 8)
    level = []
    for pair in range(PAIRS):
        staged.wait(1 + 2 * pair // UP_CUT)
        halves = [
            dot_nt(points[:, t * LEAF : (t + 1) * LEAF], basis[t])
            for t in (2 * pair, 2 * pair + 1)
        ]
        joined = jnp.concatenate(halves, axis=1).astype(BF16)
        pairs_ref[pair * COLS : (pair + 1) * COLS] = joined
        level.append(joined)
    staged.wait(len(moves) - 1)
    first = 0
    while True:
        parents = [dot_nt(joined, transfer[first + i]) for i, joined in enumerate(level)]
        first += len(level)
        if len(parents) == 1:
            break
        level = [
            jnp.concatenate(parents[i : i + 2], axis=1).astype(BF16)
            for i in range(0, len(parents), 2)
        ]
    root_ref[0] = parents[0].astype(BF16)


def upsweep(points, leaf_basis, transfer):
    return pl.pallas_call(
        up_kernel,
        in_specs=[HBM] * 3,
        out_specs=[VMEM] * 2,
        out_shape=[like((PAIRS * COLS, 2 * RANK)), like((1, COLS, RANK))],
        scratch_shapes=[
            pltpu.VMEM(points.shape, BF16),
            pltpu.VMEM(leaf_basis.shape, BF16),
            pltpu.VMEM(transfer.shape, BF16),
            pltpu.SemaphoreType.DMA((2 + LEAVES // UP_CUT,)),
        ],
        compiler_params=params(8),
        cost_estimate=cost(2**33, 2**20),
        name="upsweep",
    )(in_hbm(points), in_hbm(leaf_basis), in_hbm(transfer))


def pack_kernel(p0, p1, p2, p3, pairs_ref, after_ref, head_ref, tail_ref):
    del after_ref
    span = W * LEAF
    for row, p in enumerate((p0, p1, p2, p3)):
        rows = slice(row * COLS, (row + 1) * COLS)
        head_ref[rows, :span] = p[:, :span]
        tail_ref[rows, :span] = p[:, LEAVES * LEAF - span :]
    edge = W // 2 * COLS
    head_ref[:, span:] = pairs_ref[:edge]
    tail_ref[:, span:] = pairs_ref[PAIRS * COLS - edge :]


def pack_halos(pieces, pairs, after):
    return pl.pallas_call(
        pack_kernel,
        in_specs=[VMEM] * (SIDES + 1) + [ANY],
        out_specs=[VMEM] * 2,
        out_shape=[like((SIDES * COLS, HALO))] * 2,
        compiler_params=params(4),
        cost_estimate=cost(0, 0),
        name="pack_halos",
    )(*pieces, pairs, after)


def append_kernel(first_ref, second_ref, after_ref, out_ref):
    del after_ref
    count = first_ref.shape[0]
    out_ref[:count] = first_ref[...]
    out_ref[count:] = second_ref[...]


def append(first, second, after, weight=0):
    return pl.pallas_call(
        append_kernel,
        in_specs=[VMEM] * 2 + [ANY],
        out_specs=VMEM,
        out_shape=like((2 * first.shape[0], COLS, RANK)),
        compiler_params=params(4),
        cost_estimate=cost(weight, 0),
        name="append",
    )(first, second, after)


def near_leaf(sources, blocks_ref, t):
    wide = jnp.concatenate(sources, axis=1)
    block = jnp.concatenate(
        [blocks_ref[:, t, k].reshape(OPS * RANK, LEAF) for k in range(NEAR)], axis=1
    )
    return dot_nt(wide, block)


def store_pair(out_refs, slot, results):
    both = jnp.concatenate(results, axis=1).astype(BF16)
    for side, out_ref in enumerate(out_refs):
        out_ref[slot * COLS : (slot + 1) * COLS] = both[side * COLS : (side + 1) * COLS]


def near_kernel(offset_ref, p0, p1, p2, p3, left_ref, right_ref, blocks_ref, after_ref, *refs):
    del after_ref
    out_refs, window = refs[:SIDES], refs[SIDES]
    span, own = W * LEAF, LEAVES * LEAF
    window[:, :span] = left_ref[:, :span]
    window[:, span + own :] = right_ref[:, :span]
    for row, p in enumerate((p0, p1, p2, p3)):
        window[row * COLS : (row + 1) * COLS, span : span + own] = p[...]
    for pair in range(PAIRS):
        results = []
        for t in (2 * pair, 2 * pair + 1):
            sources = []
            for k in range(NEAR):
                start = pl.multiple_of((W + t + offset_ref[k, t]) * LEAF, LEAF)
                sources.append(window[:, pl.ds(start, LEAF)])
            results.append(near_leaf(sources, blocks_ref, t))
        store_pair(out_refs, pair, results)


def near_field(offsets, pieces, left, right, blocks, after):
    return pl.pallas_call(
        near_kernel,
        in_specs=[SMEM] + [VMEM] * 7 + [ANY],
        out_specs=[VMEM] * SIDES,
        out_shape=[like((PAIRS * COLS, 6 * RANK))] * SIDES,
        scratch_shapes=[pltpu.VMEM((SIDES * COLS, (LEAVES + 2 * W) * LEAF), BF16)],
        compiler_params=params(8),
        cost_estimate=cost(6 * 10**9, 2**22),
        name="near_field",
    )(offsets, *pieces, left, right, blocks, after)


def by_operator(flat):
    return jnp.concatenate([flat[:, o * RANK : (o + 1) * RANK] for o in range(OPS)], axis=0)


def half_of(children, odd):
    return jnp.where(odd == 1, children[:, RANK:], children[:, :RANK])


def couple_kernel(offset_ref, pairs_ref, left_ref, right_ref, coupling_ref, out_ref, near_coef):
    def spread(first, source):
        for i in range(source.shape[0] // COLS):
            both = source[i * COLS : (i + 1) * COLS, :]
            near_coef[first + 2 * i] = both[:, :RANK]
            near_coef[first + 2 * i + 1] = both[:, RANK:]

    spread(0, left_ref[:, W * LEAF :])
    spread(W, pairs_ref[...])
    spread(W + LEAVES, right_ref[:, W * LEAF :])
    for t in range(LEAVES):
        wide = jnp.concatenate([near_coef[W + t + offset_ref[k, t]] for k in range(FAR)], axis=1)
        out_ref[t] = by_operator(dot_nt(wide, coupling_ref[:, t].reshape(OPS * RANK, FAR * RANK)))


def couple_leaves(offsets, pairs, left, right, coupling):
    return pl.pallas_call(
        couple_kernel,
        in_specs=[SMEM] + [VMEM] * 4,
        out_specs=VMEM,
        out_shape=like((LEAVES, OPS * COLS, RANK), F32),
        scratch_shapes=[pltpu.VMEM((LEAVES + 2 * W, COLS, RANK), BF16)],
        compiler_params=params(8),
        cost_estimate=cost(3 * 10**9, 2**22),
        name="couple_leaves",
    )(offsets, pairs, left, right, coupling)


def far_kernel(
    where_ref,
    roots_ref,
    coupled_ref,
    root_ref,
    upper_hbm,
    top_ref,
    transfer_ref,
    basis_ref,
    out_ref,
    upper1,
    upper2,
    sems,
):
    q = where_ref[0]
    staged = Staged(
        [(upper_hbm.at[:, q >> 1], upper1), (upper_hbm.at[:, ROOTS // 2 + (q >> 2)], upper2)], sems, 2
    )

    def valid(c, height):
        return jnp.logical_and(c >= 0, c < (ROOTS >> height))

    def clip(c, height):
        return jnp.minimum(jnp.maximum(c, 0), (ROOTS >> height) - 1)

    def coef(height, c):
        if height == 0:
            return roots_ref[c - q + WINDOW // 2]
        first = (0, ROOTS // 2)[height - 1]
        joined = jnp.concatenate([coef(height - 1, 2 * c), coef(height - 1, 2 * c + 1)], axis=1)
        return dot_nt(joined, top_ref[first + c]).astype(BF16)

    def sources(height):
        c = q >> height
        odd = c % 2
        parts = []
        for even_step, odd_step in ((-2, -3), (2, -2), (3, 2)):
            other = c + jnp.where(odd == 1, odd_step, even_step)
            value = coef(height, clip(other, height))
            parts.append(jnp.where(valid(other, height), value, jnp.zeros_like(value)))
        return jnp.concatenate(parts, axis=1)

    wides = [sources(height) for height in range(TOPL)]
    staged.wait(1)
    couplings = [root_ref[:, 0], upper1[...], upper2[...]]
    fields = [
        dot_nt(wide, coupling.reshape(OPS * RANK, 3 * RANK))
        for wide, coupling in zip(wides, couplings)
    ]
    running = by_operator(fields[2])
    children = dot_nn(running.astype(BF16), top_ref[ROOTS // 2 + (q >> 2)])
    running = by_operator(fields[1]) + half_of(children, (q >> 1) % 2)
    children = dot_nn(running.astype(BF16), top_ref[q >> 1])
    running = by_operator(fields[0]) + half_of(children, q % 2)

    level = [running]
    last = LEAVES - 1
    while len(level) < LEAVES:
        count = len(level)
        last -= count
        lower = []
        for i, value in enumerate(level):
            children = dot_nn(value.astype(BF16), transfer_ref[last + i])
            lower += [children[:, :RANK], children[:, RANK:]]
        level = lower

    for t in range(LEAVES):
        far = dot_nn((level[t] + coupled_ref[t]).astype(BF16), basis_ref[t])
        out_ref[:, :, t * LEAF : (t + 1) * LEAF] = far.reshape(OPS, COLS, LEAF)


def far_field(where, roots, coupled, root_coupling, upper, top, transfer, basis):
    return pl.pallas_call(
        far_kernel,
        in_specs=[SMEM] + [VMEM] * 3 + [HBM] + [VMEM] * 3,
        out_specs=VMEM,
        out_shape=like((OPS, COLS, LEAVES * LEAF), F32),
        scratch_shapes=[
            pltpu.VMEM((OPS, RANK, 3 * RANK), BF16),
            pltpu.VMEM((OPS, RANK, 3 * RANK), BF16),
            pltpu.SemaphoreType.DMA((2,)),
        ],
        compiler_params=params(8),
        cost_estimate=cost(3 * 10**9, 2**22),
        name="far_field",
    )(where, roots, coupled, root_coupling, in_hbm(upper), top, transfer, basis)


def join_kernel(where_ref, far_ref, n0, n1, n2, n3, out_ref, ordered):
    me = where_ref[0]
    for step, near in enumerate((n0, n1, n2, n3)):
        ordered[lax.rem(me + SIDES - step, SIDES)] = near[...]
    for pair in range(PAIRS):
        parts = [ordered[r, pair * COLS : (pair + 1) * COLS].astype(F32) for r in range(SIDES)]
        for e in (0, 1):
            for o in range(OPS):
                at = (e * OPS + o) * RANK
                near = jnp.concatenate([part[:, at : at + RANK] for part in parts], axis=1)
                columns = slice((2 * pair + e) * LEAF, (2 * pair + e + 1) * LEAF)
                out_ref[o, :, columns] = (far_ref[o, :, columns] + near).astype(BF16)


def join(where, far, near):
    return pl.pallas_call(
        join_kernel,
        in_specs=[SMEM] + [VMEM] * (1 + SIDES),
        out_specs=VMEM,
        out_shape=jax.ShapeDtypeStruct((OPS, COLS, LEAVES * LEAF), BF16),
        scratch_shapes=[pltpu.VMEM((SIDES, PAIRS * COLS, 6 * RANK), BF16)],
        compiler_params=params(8),
        cost_estimate=cost(2**20, 2**22),
        name="join",
    )(where, far, *near)


def round_rhs(value, step):
    return lax.ppermute(value, "rhs", [(i, (i + step) % SIDES) for i in range(SIDES)])


def round_leaf(value, step):
    count = lax.axis_size("leaf")
    return lax.ppermute(value, "leaf", [(i, (i + step) % count) for i in range(count)])


def along_leaf(value, step):
    count = lax.axis_size("leaf")
    return lax.ppermute(
        value, "leaf", [(i, i + step) for i in range(count) if 0 <= i + step < count]
    )


def per_device(
    points,
    leaf_basis,
    local_transfer,
    top_transfer,
    leaf_coupling,
    root_coupling,
    upper_coupling,
    near_blocks,
    near_offset,
    far_offset,
):
    leaf_index = lax.axis_index("leaf").astype(jnp.int32).reshape(1)
    rhs_index = lax.axis_index("rhs").astype(jnp.int32).reshape(1)

    def grow(roots, after=None, weight=0):
        more = round_leaf(roots, -roots.shape[0])
        return append(roots, more, roots if after is None else after, weight)

    transfer = local_transfer[0]
    pieces = [points] + [round_rhs(points, -step) for step in range(1, SIDES)]
    pairs, root = upsweep(points, leaf_basis, transfer)
    roots = grow(grow(root))
    head, tail = pack_halos(pieces, pairs, root)
    left = along_leaf(tail, 1)
    right = along_leaf(head, -1)
    near = near_field(near_offset.T, pieces, left, right, near_blocks, roots)
    roots = grow(roots, None, 2**33)
    roots = grow(roots, near[0])
    near = [near[0]] + [round_rhs(near[step], step) for step in range(1, SIDES)]
    coupled = couple_leaves(far_offset.T, pairs, left, right, leaf_coupling)
    roots = append(round_leaf(roots, WINDOW // 2), roots, coupled)
    far = far_field(
        leaf_index, roots, coupled, root_coupling, upper_coupling, top_transfer, transfer, leaf_basis
    )
    return join(rhs_index, far, near)


def solution(mesh):
    placed = (
        P("rhs", "leaf"),
        P("leaf", None, None),
        P("leaf", None, None, None),
        P(),
        P(None, "leaf", None, None),
        P(None, "leaf", None, None),
        P(),
        P(None, "leaf", None, "rhs", None),
        P("leaf", None),
        P("leaf", None),
    )
    return jax.shard_map(
        per_device, mesh=mesh, in_specs=placed, out_specs=P(None, "rhs", "leaf"), check_vma=False
    )
```
